128 devices in a mesh: dp: 2 (over core), fsdp: 8 (over x, z_hi), seq: 8 (over y, z_lo).
Axes of the slice: x: 4, y: 4, z: 4 (z_hi: 2, z_lo: 2; z = z_hi * 2 + z_lo), core: 2. Of those that a mesh axis runs over, the one named last changes fastest.
Arguments:
- text: bfloat16 [2, 3072, 8192], P('dp', 'seq', 'fsdp'), may hold values from -5 to 5
- vision: bfloat16 [2, 1024, 8192], P('dp', 'seq', 'fsdp'), may hold values from -48 to 48
- cotangent: bfloat16 [2, 3072, 4096], P('dp', 'seq', 'fsdp'), may hold values from -6 to 6
- norm_gain: bfloat16 [8192], P('fsdp'), may hold values from 0.3984375 to 1.59375
- w_query: bfloat16 [8192, 4096], P('seq', 'fsdp'), may hold values from -1 to 1
- w_key: bfloat16 [8192, 1024], P('seq', 'fsdp'), may hold values from -1 to 1
- w_value: bfloat16 [8192, 1024], P('seq', 'fsdp'), may hold values from -0.0625 to 0.0625
Outputs:
- context: bfloat16 [2, 3072, 4096], P('dp', 'seq', 'fsdp')
- grad_text: bfloat16 [2, 3072, 8192], P('dp', 'seq', 'fsdp')
- grad_vision: bfloat16 [2, 1024, 8192], P('dp', 'seq', 'fsdp')
- grad_gain: float32 [8192], P('fsdp')
- grad_query: float32 [8192, 4096], P('seq', 'fsdp')
- grad_key: float32 [8192, 1024], P('seq', 'fsdp')
- grad_value: float32 [8192, 1024], P('seq', 'fsdp')
The draws below stay inside these ranges and needn't reach their ends.
All inputs are finite; a program needn't handle non-finite values.
Results may differ from the reference program's by a relative error of at most 0.033.
The reference program's roundings to bfloat16 on the way (of `normed`, `query`, `probs_low`, `grad_scores`, `query_grad`, `key_grad` and `value_grad`) count: a program that leaves them out, or rounds other values in their place, can miss the bound.
Values may be sent and summed in bfloat16 or wider, within the bound.
No kernel may reach another device: no remote copies, remote signals or barrier semaphores. Data moves between devices by JAX's collectives and lax.ppermute only.
A program may use at most 192 MiB of HBM per device.

```python
import jax
import jax.numpy as jnp
from jax import lax

D = 8192
HD = 128
HK = 8
HQ = 32
TOK_DEV = 384
IMG_DEV = 128
DV = 8192
TEXT = 3072
IMAGE = 1024
SAMPLES = 2
N_FSDP = 8
N_SEQ = 8


def base_text(key):
    text_key = jax.random.fold_in(key, 101)
    return jnp.clip(jax.random.normal(text_key, (SAMPLES, TEXT, D), jnp.float32), -5.0, 5.0)


def base_query_weight(key):
    weight_key = jax.random.fold_in(key, 202)
    values = jnp.clip(jax.random.normal(weight_key, (D, HQ * HD), jnp.float32), -5.0, 5.0)
    return values * D ** (-0.5)


def draw_text(key, part):
    return base_text(key).astype(jnp.bfloat16)


def draw_w_query(key, part):
    return base_query_weight(key).astype(jnp.bfloat16)


def draw_w_key(key, part):
    own_key = jax.random.fold_in(key, 3)
    own = jnp.clip(jax.random.normal(own_key, (DV, HK * HD), jnp.float32), -5.0, 5.0) * DV ** (-0.5)
    return own.astype(jnp.bfloat16)


def draw_vision(key, part):
    own_key = jax.random.fold_in(key, 4)
    noise_key = jax.random.fold_in(own_key, 0)
    vision = jnp.clip(jax.random.normal(noise_key, (SAMPLES, IMAGE, DV), jnp.float32), -5.0, 5.0)
    return vision.astype(jnp.bfloat16)


def steps_of(rng, dims, pieces, smallest, largest):
    def one(dim, parts):
        draws = jax.random.uniform(jax.random.fold_in(jax.random.fold_in(rng, 6), dim), (parts,), jnp.float32, smallest / len(pieces), largest / len(pieces))
        return jnp.repeat(jnp.exp(draws), dims[dim] // parts).reshape((-1,) + (1,) * (len(dims) - dim - 1))

    factor_of = one(*pieces[0])
    for cut in pieces[1:]:
        factor_of = factor_of * one(*cut)
    return factor_of


def centred(key, extent, deviation, reach, cuts=(), held_as=jnp.bfloat16):
    drawn = deviation * jax.random.normal(key, extent, jnp.float32)
    if cuts:
        drawn = drawn * steps_of(key, extent, cuts, -0.22, 0.18)
    return jnp.clip(drawn, -reach, reach).astype(held_as)


def setup_inputs(seed: int = 0) -> dict:
    seeds = jax.random.split(jax.random.key(seed), 8)
    return {
        "text": draw_text(jax.random.fold_in(seeds[7], 71), 0),
        "vision": draw_vision(jax.random.fold_in(seeds[7], 71), 0),
        "cotangent": centred(seeds[2], (SAMPLES, TEXT, HQ * HD), 1.0, 6.0, ((0, 2), (1, 8), (2, 8))),
        "norm_gain": jnp.clip(1.0 + 0.12 * jax.random.normal(seeds[3], (D,), jnp.float32), 0.3984375, 1.59375).astype(jnp.bfloat16),
        "w_query": draw_w_query(jax.random.fold_in(seeds[7], 71), 0),
        "w_key": draw_w_key(jax.random.fold_in(seeds[7], 71), 0),
        "w_value": centred(seeds[6], (DV, HK * HD), DV ** -0.5, 0.0625, ((0, 8), (1, 8))),
    }


def to_float(value):
    return value.astype(jnp.float32)

def rounded(value):
    return to_float(lax.optimization_barrier(value.astype(jnp.bfloat16)))

def attend_sample(operands):
    query_s, key_s, value_s, cot_s = operands
    group_size = HQ // HK
    softmax_scale = HD ** (-0.5)
    query_heads = to_float(query_s).reshape(TEXT, HK, group_size, HD)
    key_heads = to_float(key_s).reshape(IMAGE, HK, HD)
    value_heads = to_float(value_s).reshape(IMAGE, HK, HD)
    cot_heads = to_float(cot_s).reshape(TEXT, HK, group_size, HD)
    scores = jnp.einsum('tkgd,jkd->kgtj', query_heads, key_heads) * softmax_scale
    attn_probs = jax.nn.softmax(scores, axis=-1)
    probs_low = attn_probs.astype(jnp.bfloat16)
    context = jnp.einsum('kgtj,jkd->tkgd', to_float(probs_low), value_heads)
    context = context.astype(jnp.bfloat16).reshape(TEXT, HQ * HD)
    grad_probs = jnp.einsum('tkgd,jkd->kgtj', cot_heads, value_heads)
    row_delta = lax.optimization_barrier(jnp.sum(attn_probs * grad_probs, axis=-1, keepdims=True))
    grad_scores = (attn_probs * (grad_probs - row_delta) * softmax_scale).astype(jnp.bfloat16)
    query_grad = jnp.einsum('kgtj,jkd->tkgd', to_float(grad_scores), key_heads)
    query_grad = query_grad.astype(jnp.bfloat16).reshape(TEXT, HQ * HD)
    score_blocks = to_float(grad_scores).reshape(HK, group_size, N_SEQ, TOK_DEV, IMAGE)
    prob_blocks = to_float(probs_low).reshape(HK, group_size, N_SEQ, TOK_DEV, IMAGE)
    query_blocks = query_heads.reshape(N_SEQ, TOK_DEV, HK, group_size, HD)
    cot_blocks = cot_heads.reshape(N_SEQ, TOK_DEV, HK, group_size, HD)
    key_parts = jnp.einsum('kgbtj,btkgd->bjkd', score_blocks, query_blocks)
    value_parts = jnp.einsum('kgbtj,btkgd->bjkd', prob_blocks, cot_blocks)
    key_grad = lax.optimization_barrier(jnp.sum(rounded(key_parts), axis=0)).astype(jnp.bfloat16).reshape(IMAGE, HK * HD)
    value_grad = lax.optimization_barrier(jnp.sum(rounded(value_parts), axis=0)).astype(jnp.bfloat16).reshape(IMAGE, HK * HD)
    return (context, query_grad, key_grad, value_grad)

def reference(text, vision, cotangent, norm_gain, w_query, w_key, w_value):
    samples = text.shape[0]
    text_f = to_float(text)
    inv_rms = lax.rsqrt(lax.optimization_barrier(jnp.mean(text_f * text_f, axis=-1, keepdims=True)) + 1e-05)
    gain_f = to_float(norm_gain)
    normed = (text_f * inv_rms * gain_f).astype(jnp.bfloat16)
    normed_flat = normed.reshape(samples * TEXT, D)
    vision_flat = vision.reshape(samples * IMAGE, DV)
    query = jnp.dot(normed_flat, w_query, preferred_element_type=jnp.float32)
    query = query.astype(jnp.bfloat16).reshape(samples, TEXT, HQ * HD)
    key = jnp.dot(vision_flat, w_key, preferred_element_type=jnp.float32)
    key = key.astype(jnp.bfloat16).reshape(samples, IMAGE, HK * HD)
    value = jnp.dot(vision_flat, w_value, preferred_element_type=jnp.float32)
    value = value.astype(jnp.bfloat16).reshape(samples, IMAGE, HK * HD)
    context, query_grad, key_grad, value_grad = lax.map(attend_sample, (query, key, value, cotangent))
    flat_qgrad = query_grad.reshape(samples * TEXT, HQ * HD)
    flat_kgrad = key_grad.reshape(samples * IMAGE, HK * HD)
    flat_vgrad = value_grad.reshape(samples * IMAGE, HK * HD)
    query_cols = HQ * HD // N_FSDP
    key_cols = HK * HD // N_FSDP
    normed_grad = jnp.zeros((samples * TEXT, D), jnp.float32)
    vision_sum = jnp.zeros((samples * IMAGE, DV), jnp.float32)
    for group in range(N_FSDP):
        q_lo = group * query_cols
        k_lo = group * key_cols
        term = jnp.dot(flat_qgrad[:, q_lo:q_lo + query_cols], w_query[:, q_lo:q_lo + query_cols].T, preferred_element_type=jnp.float32)
        normed_grad = normed_grad + rounded(term)
        image_term = jnp.dot(flat_kgrad[:, k_lo:k_lo + key_cols], w_key[:, k_lo:k_lo + key_cols].T, preferred_element_type=jnp.float32)
        image_term = image_term + jnp.dot(flat_vgrad[:, k_lo:k_lo + key_cols], w_value[:, k_lo:k_lo + key_cols].T, preferred_element_type=jnp.float32)
        vision_sum = vision_sum + rounded(image_term)
    grad_vision = vision_sum.astype(jnp.bfloat16).reshape(samples, IMAGE, DV)
    grad_query = jnp.zeros((D, HQ * HD), jnp.float32)
    for block in range(samples * N_SEQ):
        rows = slice(block * TOK_DEV, (block + 1) * TOK_DEV)
        term = jnp.dot(normed_flat[rows].T, flat_qgrad[rows], preferred_element_type=jnp.float32)
        grad_query = grad_query + rounded(term)
    grad_key = jnp.zeros((DV, HK * HD), jnp.float32)
    grad_value = jnp.zeros((DV, HK * HD), jnp.float32)
    for block in range(samples * N_SEQ):
        rows = slice(block * IMG_DEV, (block + 1) * IMG_DEV)
        grad_key = grad_key + rounded(jnp.dot(vision_flat[rows].T, flat_kgrad[rows], preferred_element_type=jnp.float32))
        grad_value = grad_value + rounded(jnp.dot(vision_flat[rows].T, flat_vgrad[rows], preferred_element_type=jnp.float32))
    normed_grad = normed_grad.reshape(samples, TEXT, D)
    grad_gain = lax.optimization_barrier(jnp.sum(normed_grad * text_f * inv_rms, axis=(0, 1)))
    scaled = normed_grad * gain_f
    row_mean = lax.optimization_barrier(jnp.mean(scaled * text_f, axis=-1, keepdims=True))
    grad_text = (inv_rms * (scaled - text_f * inv_rms * inv_rms * row_mean)).astype(jnp.bfloat16)
    return (context, grad_text, grad_vision, grad_gain, grad_query, grad_key, grad_value)
```

```python
import jax
import jax.numpy as jnp
from jax import lax
from jax.experimental import pallas as pl
from jax.experimental.pallas import tpu as pltpu
from jax.sharding import PartitionSpec as P

HD = 128
EPS = 1e-05
AXES = ("dp", "fsdp", "seq")
F32 = jnp.float32
BF16 = jnp.bfloat16


def route(move):
    pairs = []
    for core in range(2):
        for x in range(4):
            for y in range(4):
                for z in range(4):
                    ids = []
                    for c2, x2, y2, z2 in ((core, x, y, z), move(core, x, y, z)):
                        ids.append((c2 * 8 + (x2 % 4) * 2 + z2 // 2) * 8 + (y2 % 4) * 2 + z2 % 2)
                    pairs.append(tuple(ids))
    return pairs


def send(value, move):
    return lax.ppermute(value, AXES, route(move))


def to_core(value):
    return send(value, lambda c, x, y, z: (1 - c, x, y, z))


def ring_of(name):
    if name == "fsdp":
        return lambda step, flip: (lambda c, x, y, z: (c, x + step, y, z ^ (2 * flip)))
    return lambda step, flip: (lambda c, x, y, z: (c, x, y + step, z ^ flip))


def block_at(name, step, flip):
    own = lax.axis_index(name)
    return ((own // 2 + step) % 4) * 2 + jnp.bitwise_xor(own % 2, flip)


def gather(value, name, place):
    move = ring_of(name)
    half = value.shape[0] // 2
    place(value, 0, 0, 0)
    other = send(value, move(0, 1))
    for flip, own in ((0, value), (1, other)):
        if flip:
            place(own, 0, flip, 0)
        left = send(own, move(1, 0))
        right = send(own, move(-1, 0))
        place(left, -1, flip, 0)
        place(right, 1, flip, 0)
        far_a = send(left[:half], move(1, 0))
        far_b = send(right[half:], move(-1, 0))
        place(far_a, 2, flip, 0)
        place(far_b, 2, flip, half)


def scatter_sum(term, name):
    move = ring_of(name)
    totals = []
    for flip in (1, 0):
        far = term(2, flip).astype(BF16)
        half = far.shape[0] // 2
        got_a = send(far[:half], move(1, 0))
        got_b = send(far[half:], move(-1, 0))
        right = term(1, flip)
        right = jnp.concatenate([right[:half] + got_a.astype(F32), right[half:]], 0)
        left = term(-1, flip)
        left = jnp.concatenate([left[:half], left[half:] + got_b.astype(F32)], 0)
        from_left = send(right.astype(BF16), move(1, 0))
        from_right = send(left.astype(BF16), move(-1, 0))
        total = term(0, flip) + from_left.astype(F32) + from_right.astype(F32)
        if flip:
            totals.append(send(total.astype(BF16), move(0, 1)).astype(F32))
        else:
            totals.append(total)
    return totals[1] + totals[0]


OFFSETS = [(step, flip) for flip in (0, 1) for step in (0, 1, -1, 2)]


def direct(values, name):
    move = ring_of(name)
    return [values[0]] + [send(v, move(*o)) for v, o in zip(values[1:], OFFSETS[1:])]


def contract(a, b, dims):
    return lax.dot_general(a, b, (dims, ((), ())), preferred_element_type=F32)


def attention_kernel(q_ref, k_ref, v_ref, cot_ref, ctx_ref, qg_ref, kg_ref, vg_ref, kacc, vacc):
    head = pl.program_id(0)
    scale = HD ** (-0.5)
    q, k, v, cot = q_ref[...], k_ref[...], v_ref[...], cot_ref[...]
    scores = contract(q, k, ((1,), (1,))) * scale
    exps = jnp.exp(scores - jnp.max(scores, axis=-1, keepdims=True))
    probs = exps / jnp.sum(exps, axis=-1, keepdims=True)
    probs_low = probs.astype(BF16)
    ctx_ref[...] = contract(probs_low, v, ((1,), (0,))).astype(BF16)
    grad_probs = contract(cot, v, ((1,), (1,)))
    row_delta = jnp.sum(probs * grad_probs, axis=-1, keepdims=True)
    grad_scores = (probs * (grad_probs - row_delta) * scale).astype(BF16)
    qg_ref[...] = contract(grad_scores, k, ((1,), (0,))).astype(BF16)
    key_term = contract(grad_scores, q, ((0,), (0,)))
    value_term = contract(probs_low, cot, ((0,), (0,)))

    @pl.when(head == 0)
    def _():
        kacc[...] = key_term
        vacc[...] = value_term

    @pl.when(head > 0)
    def _():
        kacc[...] += key_term
        vacc[...] += value_term

    @pl.when(head == pl.num_programs(0) - 1)
    def _():
        kg_ref[...] = kacc[...].astype(BF16)
        vg_ref[...] = vacc[...].astype(BF16)


def attention(query, key, value, cotangent):
    rows, width = query.shape
    images = key.shape[0]
    heads = width // HD
    per_head = pl.BlockSpec((rows, HD), lambda h: (0, h))
    shared = pl.BlockSpec((images, HD), lambda h: (0, 0))
    return pl.pallas_call(
        attention_kernel,
        grid=(heads,),
        in_specs=[per_head, shared, shared, per_head],
        out_specs=[per_head, per_head, shared, shared],
        out_shape=[
            jax.ShapeDtypeStruct((rows, width), BF16),
            jax.ShapeDtypeStruct((rows, width), BF16),
            jax.ShapeDtypeStruct((images, HD), BF16),
            jax.ShapeDtypeStruct((images, HD), BF16),
        ],
        scratch_shapes=[pltpu.VMEM((images, HD), F32), pltpu.VMEM((images, HD), F32)],
        compiler_params=pltpu.CompilerParams(vmem_limit_bytes=40 * 2**20),
        cost_estimate=pl.CostEstimate(
            flops=12 * heads * rows * images * HD,
            bytes_accessed=8 * rows * width + 8 * images * HD,
            transcendentals=heads * rows * images,
        ),
        name="attention",
    )(query, key, value, cotangent)


def per_device(text, vision, cotangent, norm_gain, w_query, w_key, w_value):
    text, vision, cotangent = text[0], vision[0], cotangent[0]
    rows, width = text.shape
    images = vision.shape[0]
    q_cols, k_cols = w_query.shape[1], w_key.shape[1]
    depth = w_query.shape[0]
    core = lax.axis_index("dp")
    text_f = text.astype(F32)
    gain_f = norm_gain.astype(F32)

    stats = jnp.concatenate([jnp.sum(text_f * text_f, axis=-1), gain_f]).reshape(-1, HD)
    stats = [s.reshape(-1) for s in direct([stats] * 8, "fsdp")]
    squares = sum(s[:rows] for s in stats)
    gains = {o: s[rows:] for o, s in zip([(-a, b) for a, b in OFFSETS], stats)}
    gains[(2, 0)], gains[(2, 1)] = gains[(-2, 0)], gains[(-2, 1)]
    inv_rms = lax.rsqrt(squares / (8 * width) + EPS)
    row_scale = jnp.concatenate([inv_rms, jnp.ones((images,), F32)])
    acts = jnp.concatenate([text, vision], 0)
    full = [jnp.zeros((rows + images, 8 * width), BF16)]

    def place_acts(block, step, flip, first):
        size = block.shape[0]
        is_text = (jnp.arange(size) + first < rows)[:, None]
        gain = jnp.where(is_text, gains[(step, flip)][None, :], 1.0)
        done = block.astype(F32) * row_scale[first:first + size, None] * gain
        at = block_at("fsdp", step, flip) * width
        full[0] = lax.dynamic_update_slice(full[0], done.astype(BF16), (first, at))

    gather(acts, "fsdp", place_acts)

    w_own = jnp.concatenate([w_query, w_key, w_value], 1)
    part = depth // 2
    weights = [jnp.zeros((8 * depth, q_cols + 2 * k_cols), BF16)]

    def place_weights(block, step, flip, first):
        at = block_at("seq", step, flip) * depth
        if (step, flip) == (0, 0):
            weights[0] = lax.dynamic_update_slice(weights[0], w_own, (at, 0))
            return
        twin = to_core(block)
        weights[0] = lax.dynamic_update_slice(weights[0], block, (at + core * part + first, 0))
        weights[0] = lax.dynamic_update_slice(weights[0], twin, (at + (1 - core) * part + first, 0))

    gather(lax.dynamic_slice_in_dim(w_own, core * part, part, 0), "seq", place_weights)
    acts_full, w_full = full[0], weights[0]

    kv_own = contract(acts_full[rows:], w_full[:, q_cols:], ((1,), (0,))).astype(BF16)
    kv_all = jnp.concatenate(direct([kv_own] * 8, "seq"), 0)
    query = contract(acts_full[:rows], w_full[:, :q_cols], ((1,), (0,))).astype(BF16)
    context, query_grad, key_part, value_part = attention(
        query, kv_all[:, :HD], kv_all[:, HD:], cotangent
    )

    kv_part = jnp.concatenate([key_part, value_part], 1).reshape(8, images, 2 * HD)
    back = {o: i for i, o in enumerate([(-a % 4, b) for a, b in OFFSETS])}
    kv_terms = direct([kv_part[back[(a % 4, b)]] for a, b in OFFSETS], "seq")
    kv_grad = sum(t.astype(F32) for t in kv_terms).astype(BF16)

    row_dot = jnp.sum(query_grad.astype(F32) * query.astype(F32), axis=-1)
    row_dots = direct([row_dot.reshape(-1, HD)] * 8, "fsdp")
    row_mean = sum(row_dots).reshape(-1) / (inv_rms * (8 * width))

    def normed_term(step, flip):
        at = block_at("fsdp", step, flip) * depth
        w = lax.dynamic_slice(w_full, (at, 0), (depth, q_cols))
        return contract(query_grad, w, ((1,), (1,)))

    def image_term(step, flip):
        at = block_at("fsdp", step, flip) * depth
        w = lax.dynamic_slice(w_full, (at, q_cols), (depth, 2 * k_cols))
        return contract(kv_grad, w, ((1,), (1,)))

    def weight_terms(first, count, grad):
        def half_of(step, flip, which):
            at = block_at("seq", step, flip) * depth + which * part
            a = lax.dynamic_slice(acts_full, (first, at), (count, part))
            return contract(a, grad, ((0,), (0,)))

        def term(step, flip):
            twin = to_core(half_of(step, flip, 1 - core).astype(BF16))
            return half_of(step, flip, core) + twin.astype(F32)

        return term

    def whole(half):
        out = jnp.zeros((depth, half.shape[1]), F32)
        out = lax.dynamic_update_slice(out, half, (core * part, 0))
        return lax.dynamic_update_slice(out, to_core(half), ((1 - core) * part, 0))

    normed_grad = scatter_sum(normed_term, "fsdp")
    grad_query = whole(scatter_sum(weight_terms(0, rows, query_grad), "seq"))
    grad_vision = scatter_sum(image_term, "fsdp").astype(BF16)
    grad_kv = whole(scatter_sum(weight_terms(rows, images, kv_grad), "seq"))

    gain_part = jnp.sum(normed_grad * text_f * inv_rms[:, None], axis=0).reshape(-1, HD)
    gain_part = gain_part + to_core(gain_part)
    move = ring_of("seq")
    gain_part = gain_part + send(gain_part, move(0, 1))
    grad_gain = (gain_part + send(gain_part, move(2, 0))) + (
        send(gain_part, move(1, 0)) + send(gain_part, move(-1, 0))
    )
    scaled = normed_grad * gain_f
    inv = inv_rms[:, None]
    grad_text = (inv * (scaled - text_f * inv * inv * row_mean[:, None])).astype(BF16)
    return (
        context[None],
        grad_text[None],
        grad_vision[None],
        grad_gain.reshape(-1),
        grad_query,
        grad_kv[:, :k_cols],
        grad_kv[:, k_cols:],
    )


def solution(mesh):
    in_specs = (
        P("dp", "seq", "fsdp"),
        P("dp", "seq", "fsdp"),
        P("dp", "seq", "fsdp"),
        P("fsdp"),
        P("seq", "fsdp"),
        P("seq", "fsdp"),
        P("seq", "fsdp"),
    )
    out_specs = (
        P("dp", "seq", "fsdp"),
        P("dp", "seq", "fsdp"),
        P("dp", "seq", "fsdp"),
        P("fsdp"),
        P("seq", "fsdp"),
        P("seq", "fsdp"),
        P("seq", "fsdp"),
    )
    return jax.shard_map(
        per_device, mesh=mesh, in_specs=in_specs, out_specs=out_specs, check_vma=False
    )
```
